32 devices in a mesh: tm: 2 (over y), space: 16 (over z, x, core).
Axes of the slice: x: 2, y: 2, z: 4, core: 2. Of those that a mesh axis runs over, the one named last changes fastest.
Arguments:
- frames_in: bfloat16 [4, 64, 128, 256], P('tm', 'space'), may hold values from -6 to 6
- w_space: bfloat16 [9, 256, 256], replicated, may hold values from -0.125 to 0.125
- w_time: bfloat16 [3, 256, 256], replicated, may hold values from -0.21875 to 0.21875
- grad_out: bfloat16 [4, 64, 128, 256], P('tm', 'space'), may hold values from -6 to 6
Outputs:
- block_out: bfloat16 [4, 64, 128, 256], P('tm', 'space')
- grad_in: bfloat16 [4, 64, 128, 256], P('tm', 'space')
- grad_space: float32 [9, 256, 256], P(None, 'tm', 'space')
- grad_time: float32 [3, 256, 256], P(None, 'tm', 'space')
The draws below stay inside these ranges and needn't reach their ends.
All inputs are finite; a program needn't handle non-finite values.
Results may differ from the reference program's by a relative error of at most 0.0057.
Values may be sent and summed in bfloat16 or wider, within the bound.
A program may use at most 64 MiB of HBM per device.

```python
import jax
import jax.numpy as jnp
from jax import lax

C = 256
COLS = 128
FRAMES = 4
ROWS = 64


def raised(values, rng, source, target, shards_of, factor):
    def block_of(dim):
        return (jnp.arange(values.shape[dim]) // (values.shape[dim] // shards_of)).reshape((-1,) + (1,) * (values.ndim - 1 - dim))

    near = jax.random.permutation(rng, shards_of)[block_of(target)]
    other_side = (block_of(target) + shards_of // 2) % shards_of
    return jnp.where((block_of(source) == near) | (block_of(source) == other_side), factor * values, values)


def steps_of(rng, dims, pieces, smallest, high):
    loudness, own = 1.0, jax.random.fold_in(rng, 6)
    for dim, blocks in pieces:
        steps = jnp.exp(jax.random.uniform(jax.random.fold_in(own, dim), (blocks,), jnp.float32, smallest / len(pieces), high / len(pieces)))
        loudness = loudness * jnp.repeat(steps, dims[dim] // blocks).reshape([-1 if axis == dim else 1 for axis in range(len(dims))])
    return loudness


def centred(own_key, extent, scale, reach, pieces=(), dtype=jnp.bfloat16):
    values = scale * jax.random.normal(own_key, extent, jnp.float32)
    if pieces:
        values = values * steps_of(own_key, extent, pieces, -0.22, 0.18)
    return jnp.clip(values, -reach, reach).astype(dtype)


def bell_draw_with(key, extent, spread, most, split, heavy, kind=jnp.bfloat16):
    drawn = spread * jax.random.normal(key, extent, jnp.float32)
    if split:
        drawn = drawn * steps_of(key, extent, split, -0.22, 0.18)
    return jnp.clip(raised(drawn, jax.random.fold_in(key, 3), *heavy), -most, most).astype(kind)


def setup_inputs(seed: int = 0) -> dict:
    streams_of = jax.random.split(jax.random.key(seed), 5)
    return {
        "frames_in": centred(streams_of[0], (FRAMES, ROWS, COLS, C), 1.0, 6.0, ((0, 2), (1, 16))),
        "w_space": centred(streams_of[1], (9, C, C), (9 * C) ** -0.5, 0.125),
        "w_time": centred(streams_of[2], (3, C, C), (3 * C) ** -0.5, 0.21875),
        "grad_out": bell_draw_with(streams_of[3], (FRAMES, ROWS, COLS, C), 1.0, 6.0, ((0, 2), (1, 16)), (1, 3, 16, 2.0)),
    }


def conv_frame(frame, w_space):
    height, width, chans = frame.shape
    padded = jnp.pad(frame, ((1, 1), (1, 1), (0, 0)))
    total = jnp.zeros((height * width, chans), jnp.float32)
    for i in range(3):
        for j in range(3):
            window = padded[i:i + height, j:j + width].reshape(-1, chans)
            total = total + jnp.dot(window, w_space[3 * i + j], preferred_element_type=jnp.float32)
    return total.reshape(height, width, chans)


def conv_back_frame(grad, w_space):
    height, width, chans = grad.shape
    padded = jnp.pad(grad, ((1, 1), (1, 1), (0, 0)))
    total = jnp.zeros((height * width, chans), jnp.float32)
    for i in range(3):
        for j in range(3):
            window = padded[2 - i:2 - i + height, 2 - j:2 - j + width].reshape(-1, chans)
            total = total + lax.dot_general(window, w_space[3 * i + j], (((1,), (1,)), ((), ())), preferred_element_type=jnp.float32)
    return total.reshape(height, width, chans)


def filter_frame(pair):
    frame, grad = pair
    height, width, chans = frame.shape
    padded = jnp.pad(frame, ((1, 1), (1, 1), (0, 0)))
    flat_grad = grad.reshape(-1, chans)
    parts = []
    for i in range(3):
        for j in range(3):
            window = padded[i:i + height, j:j + width].reshape(-1, chans)
            parts.append(lax.dot_general(window, flat_grad, (((0,), (0,)), ((), ())), preferred_element_type=jnp.float32))
    return jnp.stack(parts)


def temporal(past_ext, grad_ext, w_time, count):
    chans = past_ext.shape[-1]
    shape = grad_ext[0:count].shape
    flat_grad = grad_ext[0:count].reshape(-1, chans)
    out_sum = jnp.zeros(flat_grad.shape, jnp.float32)
    back_sum = jnp.zeros(flat_grad.shape, jnp.float32)
    filters = []
    for k in range(3):
        source = past_ext[k:k + count].reshape(-1, chans)
        out_sum = out_sum + jnp.dot(source, w_time[k], preferred_element_type=jnp.float32)
        later = grad_ext[2 - k:2 - k + count].reshape(-1, chans)
        back_sum = back_sum + lax.dot_general(later, w_time[k], (((1,), (1,)), ((), ())), preferred_element_type=jnp.float32)
        filters.append(lax.dot_general(source, flat_grad, (((0,), (0,)), ((), ())), preferred_element_type=jnp.float32))
    return out_sum.reshape(shape).astype(jnp.bfloat16), back_sum.reshape(shape).astype(jnp.bfloat16), jnp.stack(filters)


def reference(frames_in, w_space, w_time, grad_out):
    pre = lax.map(lambda frame: conv_frame(frame, w_space), frames_in)
    hidden = jax.nn.silu(pre).astype(jnp.bfloat16)
    blank = jnp.zeros((2,) + hidden.shape[1:], jnp.bfloat16)
    past_ext = jnp.concatenate([blank, hidden], axis=0)
    grad_ext = jnp.concatenate([grad_out, blank], axis=0)
    block_out, grad_hidden, grad_time = temporal(past_ext, grad_ext, w_time, hidden.shape[0])
    sig = jax.nn.sigmoid(pre)
    grad_pre = (grad_hidden.astype(jnp.float32) * sig * (1.0 + pre * (1.0 - sig))).astype(jnp.bfloat16)
    grad_in = lax.map(lambda grad: conv_back_frame(grad, w_space), grad_pre).astype(jnp.bfloat16)
    grad_space = jnp.sum(lax.map(filter_frame, (frames_in, grad_pre)), axis=0)
    return block_out, grad_in, grad_space, grad_time
```

```python
import jax
import jax.numpy as jnp
from jax import lax
from jax.sharding import PartitionSpec as P


def extended_2(block, sides, width):
    for axis, dim in sides:
        count = lax.axis_size(axis)
        forward = [(i, i + 1) for i in range(count - 1)]
        backward = [(target, source) for source, target in forward]
        low = lax.ppermute(
            lax.slice_in_dim(block, block.shape[dim] - width, None, axis=dim), axis, forward
        )
        high = lax.ppermute(lax.slice_in_dim(block, 0, width, axis=dim), axis, backward)
        block = jnp.concatenate([low, block, high], axis=dim)
    return block


def pad_columns(field):
    return jnp.pad(field, ((0, 0), (0, 0), (1, 1), (0, 0)))


def temporal_forward(past_ext, grad, w_time):
    count, chans = grad.shape[0], grad.shape[-1]
    flat_grad = grad.reshape(-1, chans)
    out_sum = jnp.zeros(flat_grad.shape, jnp.float32)
    filters = []
    for k in range(3):
        source = past_ext[k : k + count].reshape(-1, chans)
        out_sum = out_sum + jnp.dot(source, w_time[k], preferred_element_type=jnp.float32)
        filters.append(
            lax.dot_general(
                flat_grad, source, (((0,), (0,)), ((), ())), preferred_element_type=jnp.float32
            )
        )
    return out_sum.reshape(grad.shape).astype(jnp.bfloat16), filters


def temporal_backward(grad_ext, w_time, count):
    chans = grad_ext.shape[-1]
    back_sum = jnp.zeros((grad_ext[0:count].size // chans, chans), jnp.float32)
    for k in range(3):
        later = grad_ext[2 - k : 2 - k + count].reshape(-1, chans)
        back_sum = back_sum + lax.dot_general(
            later, w_time[k], (((1,), (1,)), ((), ())), preferred_element_type=jnp.float32
        )
    return back_sum.reshape(grad_ext[0:count].shape).astype(jnp.bfloat16)


def exchange(keep, send, axis, step):
    count = lax.axis_size(axis)
    got = lax.ppermute(send.astype(jnp.bfloat16), axis, [(i, i ^ step) for i in range(count)])
    return keep + got.astype(jnp.float32)


def halve_chunks(sums, axis, step):
    taps, chunks, rows, width = sums.shape
    pairs = sums.reshape(taps, chunks // 2, 2, rows, width)
    mine = lax.rem(lax.axis_index(axis) // step, 2)
    keep = lax.dynamic_index_in_dim(pairs, mine, 2, keepdims=False)
    send = lax.dynamic_index_in_dim(pairs, 1 - mine, 2, keepdims=False)
    return exchange(keep, send, axis, step)


def halve_width(sums, axis, step):
    half = sums.shape[3] // 2
    mine = lax.rem(lax.axis_index(axis) // step, 2)
    low, high = sums[..., :half], sums[..., half:]
    keep = jnp.where(mine == 0, low, high)
    send = jnp.where(mine == 0, high, low)
    return exchange(keep, send, axis, step)


def scatter_sums(sums):
    bands, groups = lax.axis_size("space"), lax.axis_size("tm")
    taps, rows, width = sums.shape
    sums = sums.reshape(taps, bands, rows // bands, width)
    sums = halve_chunks(sums, "space", 1)
    step = groups // 2
    while step >= 1:
        sums = halve_width(sums, "tm", step)
        step //= 2
    step = 2
    while step < bands:
        sums = halve_chunks(sums, "space", step)
        step *= 2
    return jnp.transpose(sums[:, 0], (0, 2, 1))


def body(frames_in, w_space, w_time, grad_out):
    count, height, width, chans = frames_in.shape
    groups = lax.axis_size("tm")
    onward = [(i, i + 1) for i in range(groups - 1)]
    grad_next = lax.ppermute(grad_out[:2], "tm", [(t, s) for s, t in onward])
    extended = pad_columns(extended_2(frames_in, (("space", 1),), 1))
    pre = jnp.zeros((count * height * width, chans), jnp.float32)
    for i in range(3):
        for j in range(3):
            window = extended[:, i : i + height, j : j + width].reshape(-1, chans)
            pre = pre + jnp.dot(window, w_space[3 * i + j], preferred_element_type=jnp.float32)
    pre = pre.reshape(count, height, width, chans)
    hidden = jax.nn.silu(pre).astype(jnp.bfloat16)
    past = lax.ppermute(hidden[count - 2 :], "tm", onward)
    grad_hidden = temporal_backward(
        jnp.concatenate([grad_out, grad_next], axis=0), w_time, count
    )
    sig = jax.nn.sigmoid(pre)
    grad_pre = (grad_hidden.astype(jnp.float32) * sig * (1.0 + pre * (1.0 - sig))).astype(
        jnp.bfloat16
    )
    grad_ext_rows = pad_columns(extended_2(grad_pre, (("space", 1),), 1))
    flat_pre = grad_pre.reshape(-1, chans)
    terms = []
    for i in range(3):
        for j in range(3):
            source = extended[:, i : i + height, j : j + width].reshape(-1, chans)
            terms.append(
                lax.dot_general(
                    flat_pre, source, (((0,), (0,)), ((), ())), preferred_element_type=jnp.float32
                )
            )
    block_out, time_terms = temporal_forward(
        jnp.concatenate([past, hidden], axis=0), grad_out, w_time
    )
    owned = scatter_sums(jnp.stack(terms + time_terms))
    back = jnp.zeros((count * height * width, chans), jnp.float32)
    for i in range(3):
        for j in range(3):
            window = grad_ext_rows[:, 2 - i : 2 - i + height, 2 - j : 2 - j + width].reshape(
                -1, chans
            )
            back = back + lax.dot_general(
                window,
                w_space[3 * i + j],
                (((1,), (1,)), ((), ())),
                preferred_element_type=jnp.float32,
            )
    grad_in = back.reshape(count, height, width, chans).astype(jnp.bfloat16)
    return (block_out, grad_in, owned[:9], owned[9:])


def solution(mesh):
    in_specs = (P("tm", "space", None, None), P(), P(), P("tm", "space", None, None))
    out_specs = (
        P("tm", "space", None, None),
        P("tm", "space", None, None),
        P(None, "tm", "space"),
        P(None, "tm", "space"),
    )
    return jax.shard_map(body, mesh=mesh, in_specs=in_specs, out_specs=out_specs, check_vma=False)
```

```python
import functools

import jax
import jax.numpy as jnp
from jax import lax
from jax.experimental import pallas as pl
from jax.experimental.pallas import tpu as pltpu
from jax.sharding import PartitionSpec as P


def extended_2(block, sides, width):
    for axis, dim in sides:
        count = lax.axis_size(axis)
        forward = [(i, i + 1) for i in range(count - 1)]
        backward = [(target, source) for source, target in forward]
        low = lax.ppermute(
            lax.slice_in_dim(block, block.shape[dim] - width, None, axis=dim), axis, forward
        )
        high = lax.ppermute(lax.slice_in_dim(block, 0, width, axis=dim), axis, backward)
        block = jnp.concatenate([low, block, high], axis=dim)
    return block


def pad_columns(field):
    return jnp.pad(field, ((0, 0), (0, 0), (1, 1), (0, 0)))


def temporal_forward(past_ext, grad, w_time):
    count, chans = grad.shape[0], grad.shape[-1]
    flat_grad = grad.reshape(-1, chans)
    out_sum = jnp.zeros(flat_grad.shape, jnp.float32)
    filters = []
    for k in range(3):
        source = past_ext[k : k + count].reshape(-1, chans)
        out_sum = out_sum + jnp.dot(source, w_time[k], preferred_element_type=jnp.float32)
        filters.append(
            lax.dot_general(
                flat_grad, source, (((0,), (0,)), ((), ())), preferred_element_type=jnp.float32
            )
        )
    return out_sum.reshape(grad.shape).astype(jnp.bfloat16), filters


def temporal_backward(grad_ext, w_time, count):
    chans = grad_ext.shape[-1]
    back_sum = jnp.zeros((grad_ext[0:count].size // chans, chans), jnp.float32)
    for k in range(3):
        later = grad_ext[2 - k : 2 - k + count].reshape(-1, chans)
        back_sum = back_sum + lax.dot_general(
            later, w_time[k], (((1,), (1,)), ((), ())), preferred_element_type=jnp.float32
        )
    return back_sum.reshape(grad_ext[0:count].shape).astype(jnp.bfloat16)


MESH = pl.DeviceIdType.MESH


def bit_orders(bands, groups):
    frame_bits = [("tm", 1 << i, 1 << i) for i in range(groups.bit_length() - 1)]
    row_bits = [("space", 1 << i, groups << i) for i in range(bands.bit_length() - 1)]
    first, second, rest = row_bits[:1], row_bits[1:2], row_bits[2:]
    return [
        first + frame_bits + second + rest,
        first + second + rest + frame_bits,
        first + rest + frame_bits + second,
    ]


def side(bit):
    axis, step, _ = bit
    return lax.rem(lax.axis_index(axis) // step, 2)


def partner(bit):
    axis, step, _ = bit
    at = {"tm": lax.axis_index("tm"), "space": lax.axis_index("space")}
    at[axis] = at[axis] + step - 2 * step * side(bit)
    return (at["tm"], at["space"])


def each(count, step):
    if count <= 16:
        for e in range(count):
            step(e)
    else:
        lax.fori_loop(0, count, lambda e, carry: (step(e), carry)[1], 0)


def spread(e, free):
    if isinstance(e, int):
        return sum(((e >> i) % 2) * bit[2] for i, bit in enumerate(free))
    total = 0
    for i, bit in enumerate(free):
        total = total + lax.rem(e // (1 << i), 2) * bit[2]
    return total


def scatter_kernel(orders, sums_ref, out_ref, total, sent, landed, send_sems, recv_sems):
    parts = len(orders)
    rows = sums_ref.shape[1] // parts
    stages = len(orders[0])
    barrier = pltpu.get_barrier_semaphore()
    for bit in orders[0]:
        pl.semaphore_signal(barrier, inc=1, device_id=partner(bit), device_id_type=MESH)
    pl.semaphore_wait(barrier, stages)

    def span(part):
        return pl.ds(part * rows, rows)

    def start_of(stage):
        return sum(1 << (stages - 1 - s) for s in range(stage))

    def fixed(part, stage):
        return sum(side(bit) * bit[2] for bit in orders[part][:stage])

    def send(part, stage):
        bit, free = orders[part][stage], orders[part][stage + 1 :]
        count, start = 1 << len(free), start_of(stage)
        base = fixed(part, stage) + (1 - side(bit)) * bit[2]
        source = sums_ref if stage == 0 else total

        def pack(e):
            block = source[base + spread(e, free), span(part), :]
            sent[part, start + e] = block.astype(jnp.bfloat16)

        each(count, pack)
        copy = pltpu.make_async_remote_copy(
            src_ref=sent.at[part, pl.ds(start, count)],
            dst_ref=landed.at[part, pl.ds(start, count)],
            send_sem=send_sems.at[part, stage],
            recv_sem=recv_sems.at[part, stage],
            device_id=partner(bit),
            device_id_type=MESH,
        )
        copy.start()
        return copy

    def add(part, stage):
        free = orders[part][stage + 1 :]
        count, start = 1 << len(free), start_of(stage)
        base = fixed(part, stage + 1)
        source = sums_ref if stage == 0 else total

        def step(e):
            at = base + spread(e, free)
            got = landed[part, start + e].astype(jnp.float32)
            total[at, span(part), :] = source[at, span(part), :] + got

        each(count, step)

    copies = [send(part, 0) for part in range(parts)]
    for stage in range(stages):
        for part in range(parts):
            copies[part].wait_recv()
            add(part, stage)
            copies[part].wait_send()
            if stage + 1 < stages:
                copies[part] = send(part, stage + 1)
            else:
                out_ref[span(part), :] = total[fixed(part, stages), span(part), :]


def scatter_sums(sums):
    bands, groups = lax.axis_size("space"), lax.axis_size("tm")
    taps, rows, width = sums.shape
    depth, lanes = rows // bands, width // groups
    size = taps * depth * lanes
    blocks = sums.reshape(taps, bands, depth, groups, lanes).transpose(1, 3, 0, 2, 4)
    blocks = blocks.reshape(bands * groups, size // 128, 128)
    lines = -(-size // 128 // 16) * 16
    blocks = jnp.pad(blocks, ((0, 0), (0, lines - size // 128), (0, 0)))
    orders = bit_orders(bands, groups)
    if lines % 48:
        orders = orders[:1]
    parts, stages, devices = len(orders), len(orders[0]), bands * groups
    owned = pl.pallas_call(
        functools.partial(scatter_kernel, orders),
        out_shape=jax.ShapeDtypeStruct((lines, 128), jnp.float32),
        in_specs=[pl.BlockSpec(memory_space=pltpu.VMEM)],
        out_specs=pl.BlockSpec(memory_space=pltpu.VMEM),
        scratch_shapes=[
            pltpu.VMEM((devices, lines, 128), jnp.float32),
            pltpu.VMEM((parts, devices, lines // parts, 128), jnp.bfloat16),
            pltpu.VMEM((parts, devices, lines // parts, 128), jnp.bfloat16),
            pltpu.SemaphoreType.DMA((parts, stages)),
            pltpu.SemaphoreType.DMA((parts, stages)),
        ],
        compiler_params=pltpu.CompilerParams(
            collective_id=0, has_side_effects=True, vmem_limit_bytes=24 * 1024 * 1024
        ),
    )(blocks)
    owned = owned[: size // 128].reshape(taps, depth, lanes)
    return jnp.transpose(owned, (0, 2, 1))


def body(frames_in, w_space, w_time, grad_out):
    count, height, width, chans = frames_in.shape
    groups = lax.axis_size("tm")
    onward = [(i, i + 1) for i in range(groups - 1)]
    grad_next = lax.ppermute(grad_out[:2], "tm", [(t, s) for s, t in onward])
    extended = pad_columns(extended_2(frames_in, (("space", 1),), 1))
    pre = jnp.zeros((count * height * width, chans), jnp.float32)
    for i in range(3):
        for j in range(3):
            window = extended[:, i : i + height, j : j + width].reshape(-1, chans)
            pre = pre + jnp.dot(window, w_space[3 * i + j], preferred_element_type=jnp.float32)
    pre = pre.reshape(count, height, width, chans)
    hidden = jax.nn.silu(pre).astype(jnp.bfloat16)
    past = lax.ppermute(hidden[count - 2 :], "tm", onward)
    grad_hidden = temporal_backward(
        jnp.concatenate([grad_out, grad_next], axis=0), w_time, count
    )
    sig = jax.nn.sigmoid(pre)
    grad_pre = (grad_hidden.astype(jnp.float32) * sig * (1.0 + pre * (1.0 - sig))).astype(
        jnp.bfloat16
    )
    grad_ext_rows = pad_columns(extended_2(grad_pre, (("space", 1),), 1))
    flat_pre = grad_pre.reshape(-1, chans)
    terms = []
    for i in range(3):
        for j in range(3):
            source = extended[:, i : i + height, j : j + width].reshape(-1, chans)
            terms.append(
                lax.dot_general(
                    flat_pre, source, (((0,), (0,)), ((), ())), preferred_element_type=jnp.float32
                )
            )
    block_out, time_terms = temporal_forward(
        jnp.concatenate([past, hidden], axis=0), grad_out, w_time
    )
    owned = scatter_sums(jnp.stack(terms + time_terms))
    back = jnp.zeros((count * height * width, chans), jnp.float32)
    for i in range(3):
        for j in range(3):
            window = grad_ext_rows[:, 2 - i : 2 - i + height, 2 - j : 2 - j + width].reshape(
                -1, chans
            )
            back = back + lax.dot_general(
                window,
                w_space[3 * i + j],
                (((1,), (1,)), ((), ())),
                preferred_element_type=jnp.float32,
            )
    grad_in = back.reshape(count, height, width, chans).astype(jnp.bfloat16)
    return (block_out, grad_in, owned[:9], owned[9:])


def solution(mesh):
    in_specs = (P("tm", "space", None, None), P(), P(), P("tm", "space", None, None))
    out_specs = (
        P("tm", "space", None, None),
        P("tm", "space", None, None),
        P(None, "tm", "space"),
        P(None, "tm", "space"),
    )
    return jax.shard_map(body, mesh=mesh, in_specs=in_specs, out_specs=out_specs, check_vma=False)
```

```python
import functools

import jax
import jax.numpy as jnp
from jax import lax
from jax.experimental import pallas as pl
from jax.experimental.pallas import tpu as pltpu
from jax.sharding import PartitionSpec as P


def extended_2(block, sides, width):
    for axis, dim in sides:
        count = lax.axis_size(axis)
        forward = [(i, i + 1) for i in range(count - 1)]
        backward = [(target, source) for source, target in forward]
        low = lax.ppermute(
            lax.slice_in_dim(block, block.shape[dim] - width, None, axis=dim), axis, forward
        )
        high = lax.ppermute(lax.slice_in_dim(block, 0, width, axis=dim), axis, backward)
        block = jnp.concatenate([low, block, high], axis=dim)
    return block


def pad_columns(field):
    return jnp.pad(field, ((0, 0), (0, 0), (1, 1), (0, 0)))


def temporal_forward(past_ext, grad, w_time):
    count, chans = grad.shape[0], grad.shape[-1]
    flat_grad = grad.reshape(-1, chans)
    out_sum = jnp.zeros(flat_grad.shape, jnp.float32)
    filters = []
    for k in range(3):
        source = past_ext[k : k + count].reshape(-1, chans)
        out_sum = out_sum + jnp.dot(source, w_time[k], preferred_element_type=jnp.float32)
        filters.append(
            lax.dot_general(
                flat_grad, source, (((0,), (0,)), ((), ())), preferred_element_type=jnp.float32
            )
        )
    return out_sum.reshape(grad.shape).astype(jnp.bfloat16), filters


def temporal_backward(grad_ext, w_time, count):
    chans = grad_ext.shape[-1]
    back_sum = jnp.zeros((grad_ext[0:count].size // chans, chans), jnp.float32)
    for k in range(3):
        later = grad_ext[2 - k : 2 - k + count].reshape(-1, chans)
        back_sum = back_sum + lax.dot_general(
            later, w_time[k], (((1,), (1,)), ((), ())), preferred_element_type=jnp.float32
        )
    return back_sum.reshape(grad_ext[0:count].shape).astype(jnp.bfloat16)


MESH = pl.DeviceIdType.MESH


def bit_orders(bands, groups):
    frame_bits = [("tm", 1 << i, 1 << i) for i in range(groups.bit_length() - 1)]
    row_bits = [("space", 1 << i, groups << i) for i in range(bands.bit_length() - 1)]
    first, second, rest = row_bits[:1], row_bits[1:2], row_bits[2:]
    return [
        first + frame_bits + second + rest,
        first + second + rest + frame_bits,
        first + rest + frame_bits + second,
    ]


def side(bit):
    axis, step, _ = bit
    return lax.rem(lax.axis_index(axis) // step, 2)


def partner(bit):
    axis, step, _ = bit
    at = {"tm": lax.axis_index("tm"), "space": lax.axis_index("space")}
    at[axis] = at[axis] + step - 2 * step * side(bit)
    return (at["tm"], at["space"])


def each(count, step):
    if count <= 16:
        for e in range(count):
            step(e)
    else:
        lax.fori_loop(0, count, lambda e, carry: (step(e), carry)[1], 0)


def spread(e, free):
    if isinstance(e, int):
        return sum(((e >> i) % 2) * bit[2] for i, bit in enumerate(free))
    total = 0
    for i, bit in enumerate(free):
        total = total + lax.rem(e // (1 << i), 2) * bit[2]
    return total


def scatter_kernel(orders, depth, lanes, *refs):
    taps = len(refs) - 6
    tap_refs = refs[:taps]
    out_ref, total, sent, landed, send_sems, recv_sems = refs[taps:]
    parts = len(orders)
    group = taps // parts
    rows = group * depth
    groups = lax.axis_size("tm")
    stages = len(orders[0])
    barrier = pltpu.get_barrier_semaphore()
    for bit in orders[0]:
        pl.semaphore_signal(barrier, inc=1, device_id=partner(bit), device_id_type=MESH)
    pl.semaphore_wait(barrier, stages)

    def span(part):
        return pl.ds(part * rows, rows)

    def tap_block(part, k, at):
        down = pl.multiple_of((at // groups) * depth, depth)
        across = pl.multiple_of(lax.rem(at, groups) * lanes, lanes)
        return tap_refs[part * group + k][pl.ds(down, depth), pl.ds(across, lanes)]

    def start_of(stage):
        return sum(1 << (stages - 1 - s) for s in range(stage))

    def fixed(part, stage):
        return sum(side(bit) * bit[2] for bit in orders[part][:stage])

    def send(part, stage):
        bit, free = orders[part][stage], orders[part][stage + 1 :]
        count, start = 1 << len(free), start_of(stage)
        base = fixed(part, stage) + (1 - side(bit)) * bit[2]

        def pack(e):
            at = base + spread(e, free)
            if stage == 0:
                for k in range(group):
                    block = tap_block(part, k, at)
                    sent[part, start + e, pl.ds(k * depth, depth), :] = block.astype(jnp.bfloat16)
            else:
                sent[part, start + e] = total[at, span(part), :].astype(jnp.bfloat16)

        each(count, pack)
        copy = pltpu.make_async_remote_copy(
            src_ref=sent.at[part, pl.ds(start, count)],
            dst_ref=landed.at[part, pl.ds(start, count)],
            send_sem=send_sems.at[part, stage],
            recv_sem=recv_sems.at[part, stage],
            device_id=partner(bit),
            device_id_type=MESH,
        )
        copy.start()
        return copy

    def add(part, stage):
        free = orders[part][stage + 1 :]
        count, start = 1 << len(free), start_of(stage)
        base = fixed(part, stage + 1)

        def step(e):
            at = base + spread(e, free)
            if stage == 0:
                for k in range(group):
                    here = pl.ds(k * depth, depth)
                    got = landed[part, start + e, here, :].astype(jnp.float32)
                    mine = pl.ds(part * rows + k * depth, depth)
                    total[at, mine, :] = tap_block(part, k, at) + got
            else:
                got = landed[part, start + e].astype(jnp.float32)
                total[at, span(part), :] = total[at, span(part), :] + got

        each(count, step)

    copies = [send(part, 0) for part in range(parts)]
    for stage in range(stages):
        for part in range(parts):
            copies[part].wait_recv()
            add(part, stage)
            copies[part].wait_send()
            if stage + 1 < stages:
                copies[part] = send(part, stage + 1)
            else:
                out_ref[span(part), :] = total[fixed(part, stages), span(part), :]


def exchange(keep, send, axis, step):
    count = lax.axis_size(axis)
    got = lax.ppermute(send.astype(jnp.bfloat16), axis, [(i, i ^ step) for i in range(count)])
    return keep + got.astype(jnp.float32)


def halve_chunks(sums, axis, step):
    taps, chunks, rows, width = sums.shape
    pairs = sums.reshape(taps, chunks // 2, 2, rows, width)
    mine = lax.rem(lax.axis_index(axis) // step, 2)
    keep = lax.dynamic_index_in_dim(pairs, mine, 2, keepdims=False)
    send = lax.dynamic_index_in_dim(pairs, 1 - mine, 2, keepdims=False)
    return exchange(keep, send, axis, step)


def halve_width(sums, axis, step):
    half = sums.shape[3] // 2
    mine = lax.rem(lax.axis_index(axis) // step, 2)
    low, high = sums[..., :half], sums[..., half:]
    keep = jnp.where(mine == 0, low, high)
    send = jnp.where(mine == 0, high, low)
    return exchange(keep, send, axis, step)


def scatter_by_permutes(sums):
    bands, groups = lax.axis_size("space"), lax.axis_size("tm")
    taps, rows, width = sums.shape
    sums = sums.reshape(taps, bands, rows // bands, width)
    sums = halve_chunks(sums, "space", 1)
    step = groups // 2
    while step >= 1:
        sums = halve_width(sums, "tm", step)
        step //= 2
    step = 2
    while step < bands:
        sums = halve_chunks(sums, "space", step)
        step *= 2
    return jnp.transpose(sums[:, 0], (0, 2, 1))


def scatter_sums(terms):
    bands, groups = lax.axis_size("space"), lax.axis_size("tm")
    taps, (rows, width) = len(terms), terms[0].shape
    depth, lanes = rows // bands, width // groups
    if depth % 16 or lanes != 128 or taps % 3:
        return scatter_by_permutes(jnp.stack(terms))
    orders = bit_orders(bands, groups)
    parts, stages, devices = len(orders), len(orders[0]), bands * groups
    lines = taps * depth
    owned = pl.pallas_call(
        functools.partial(scatter_kernel, orders, depth, lanes),
        out_shape=jax.ShapeDtypeStruct((lines, 128), jnp.float32),
        in_specs=[pl.BlockSpec(memory_space=pltpu.VMEM)] * taps,
        out_specs=pl.BlockSpec(memory_space=pltpu.VMEM),
        scratch_shapes=[
            pltpu.VMEM((devices, lines, 128), jnp.float32),
            pltpu.VMEM((parts, devices, lines // parts, 128), jnp.bfloat16),
            pltpu.VMEM((parts, devices, lines // parts, 128), jnp.bfloat16),
            pltpu.SemaphoreType.DMA((parts, stages)),
            pltpu.SemaphoreType.DMA((parts, stages)),
        ],
        compiler_params=pltpu.CompilerParams(
            collective_id=0, has_side_effects=True, vmem_limit_bytes=16 * 1024 * 1024
        ),
    )(*terms)
    return jnp.transpose(owned.reshape(taps, depth, lanes), (0, 2, 1))


def body(frames_in, w_space, w_time, grad_out):
    count, height, width, chans = frames_in.shape
    groups = lax.axis_size("tm")
    onward = [(i, i + 1) for i in range(groups - 1)]
    grad_next = lax.ppermute(grad_out[:2], "tm", [(t, s) for s, t in onward])
    extended = pad_columns(extended_2(frames_in, (("space", 1),), 1))
    pre = jnp.zeros((count * height * width, chans), jnp.float32)
    for i in range(3):
        for j in range(3):
            window = extended[:, i : i + height, j : j + width].reshape(-1, chans)
            pre = pre + jnp.dot(window, w_space[3 * i + j], preferred_element_type=jnp.float32)
    pre = pre.reshape(count, height, width, chans)
    hidden = jax.nn.silu(pre).astype(jnp.bfloat16)
    past = lax.ppermute(hidden[count - 2 :], "tm", onward)
    grad_hidden = temporal_backward(
        jnp.concatenate([grad_out, grad_next], axis=0), w_time, count
    )
    sig = jax.nn.sigmoid(pre)
    grad_pre = (grad_hidden.astype(jnp.float32) * sig * (1.0 + pre * (1.0 - sig))).astype(
        jnp.bfloat16
    )
    grad_ext_rows = pad_columns(extended_2(grad_pre, (("space", 1),), 1))
    flat_pre = grad_pre.reshape(-1, chans)
    terms = []
    for i in range(3):
        for j in range(3):
            source = extended[:, i : i + height, j : j + width].reshape(-1, chans)
            terms.append(
                lax.dot_general(
                    flat_pre, source, (((0,), (0,)), ((), ())), preferred_element_type=jnp.float32
                )
            )
    block_out, time_terms = temporal_forward(
        jnp.concatenate([past, hidden], axis=0), grad_out, w_time
    )
    owned = scatter_sums(terms + time_terms)
    back = jnp.zeros((count * height * width, chans), jnp.float32)
    for i in range(3):
        for j in range(3):
            window = grad_ext_rows[:, 2 - i : 2 - i + height, 2 - j : 2 - j + width].reshape(
                -1, chans
            )
            back = back + lax.dot_general(
                window,
                w_space[3 * i + j],
                (((1,), (1,)), ((), ())),
                preferred_element_type=jnp.float32,
            )
    grad_in = back.reshape(count, height, width, chans).astype(jnp.bfloat16)
    return (block_out, grad_in, owned[:9], owned[9:])


def solution(mesh):
    in_specs = (P("tm", "space", None, None), P(), P(), P("tm", "space", None, None))
    out_specs = (
        P("tm", "space", None, None),
        P("tm", "space", None, None),
        P(None, "tm", "space"),
        P(None, "tm", "space"),
    )
    return jax.shard_map(body, mesh=mesh, in_specs=in_specs, out_specs=out_specs, check_vma=False)
```

```python
import functools

import jax
import jax.numpy as jnp
from jax import lax
from jax.experimental import pallas as pl
from jax.experimental.layout import Layout, with_layout_constraint
from jax.experimental.pallas import tpu as pltpu
from jax.sharding import PartitionSpec as P


def extended_2(block, sides, width):
    for axis, dim in sides:
        count = lax.axis_size(axis)
        forward = [(i, i + 1) for i in range(count - 1)]
        backward = [(target, source) for source, target in forward]
        low = lax.ppermute(
            lax.slice_in_dim(block, block.shape[dim] - width, None, axis=dim), axis, forward
        )
        high = lax.ppermute(lax.slice_in_dim(block, 0, width, axis=dim), axis, backward)
        block = jnp.concatenate([low, block, high], axis=dim)
    return block


def pad_columns(field):
    return jnp.pad(field, ((0, 0), (0, 0), (1, 1), (0, 0)))


def temporal_forward(past_ext, grad, w_time):
    count, chans = grad.shape[0], grad.shape[-1]
    flat_grad = grad.reshape(-1, chans)
    out_sum = jnp.zeros(flat_grad.shape, jnp.float32)
    filters = []
    for k in range(3):
        source = past_ext[k : k + count].reshape(-1, chans)
        out_sum = out_sum + jnp.dot(source, w_time[k], preferred_element_type=jnp.float32)
        filters.append(
            lax.dot_general(
                flat_grad, source, (((0,), (0,)), ((), ())), preferred_element_type=jnp.float32
            )
        )
    return out_sum.reshape(grad.shape).astype(jnp.bfloat16), filters


def temporal_backward(grad_ext, w_time, count):
    chans = grad_ext.shape[-1]
    back_sum = jnp.zeros((grad_ext[0:count].size // chans, chans), jnp.float32)
    for k in range(3):
        later = grad_ext[2 - k : 2 - k + count].reshape(-1, chans)
        back_sum = back_sum + lax.dot_general(
            later, w_time[k], (((1,), (1,)), ((), ())), preferred_element_type=jnp.float32
        )
    return back_sum.reshape(grad_ext[0:count].shape).astype(jnp.bfloat16)


MESH = pl.DeviceIdType.MESH


def rows_major(field):
    return with_layout_constraint(field, Layout(tuple(range(field.ndim))))


def bit_orders(bands, groups):
    frame_bits = [("tm", 1 << i, 1 << i) for i in range(groups.bit_length() - 1)]
    row_bits = [("space", 1 << i, groups << i) for i in range(bands.bit_length() - 1)]
    first, second, rest = row_bits[:1], row_bits[1:2], row_bits[2:]
    return [
        first + frame_bits + second + rest,
        first + second + rest + frame_bits,
        first + rest + frame_bits + second,
    ]


def side(bit):
    axis, step, _ = bit
    return lax.rem(lax.axis_index(axis) // step, 2)


def partner(bit):
    axis, step, _ = bit
    at = {"tm": lax.axis_index("tm"), "space": lax.axis_index("space")}
    at[axis] = at[axis] + step - 2 * step * side(bit)
    return (at["tm"], at["space"])


def each(count, step):
    if count <= 16:
        for e in range(count):
            step(e)
    else:
        lax.fori_loop(0, count, lambda e, carry: (step(e), carry)[1], 0)


def spread(e, free):
    if isinstance(e, int):
        return sum(((e >> i) % 2) * bit[2] for i, bit in enumerate(free))
    total = 0
    for i, bit in enumerate(free):
        total = total + lax.rem(e // (1 << i), 2) * bit[2]
    return total


def scatter_kernel(orders, depth, lanes, *refs):
    taps = len(refs) - 6
    tap_refs = refs[:taps]
    out_ref, total, sent, landed, send_sems, recv_sems = refs[taps:]
    parts = len(orders)
    group = taps // parts
    rows = group * depth
    groups = lax.axis_size("tm")
    stages = len(orders[0])
    barrier = pltpu.get_barrier_semaphore()
    for bit in orders[0]:
        pl.semaphore_signal(barrier, inc=1, device_id=partner(bit), device_id_type=MESH)
    pl.semaphore_wait(barrier, stages)

    def span(part):
        return pl.ds(part * rows, rows)

    def tap_block(part, k, at):
        down = pl.multiple_of((at // groups) * depth, depth)
        across = pl.multiple_of(lax.rem(at, groups) * lanes, lanes)
        return tap_refs[part * group + k][pl.ds(down, depth), pl.ds(across, lanes)]

    def start_of(stage):
        return sum(1 << (stages - 1 - s) for s in range(stage))

    def fixed(part, stage):
        return sum(side(bit) * bit[2] for bit in orders[part][:stage])

    def send(part, stage):
        bit, free = orders[part][stage], orders[part][stage + 1 :]
        count, start = 1 << len(free), start_of(stage)
        base = fixed(part, stage) + (1 - side(bit)) * bit[2]

        def pack(e):
            at = base + spread(e, free)
            if stage == 0:
                for k in range(group):
                    block = tap_block(part, k, at)
                    sent[part, start + e, pl.ds(k * depth, depth), :] = block.astype(jnp.bfloat16)
            else:
                sent[part, start + e] = total[at, span(part), :].astype(jnp.bfloat16)

        each(count, pack)
        copy = pltpu.make_async_remote_copy(
            src_ref=sent.at[part, pl.ds(start, count)],
            dst_ref=landed.at[part, pl.ds(start, count)],
            send_sem=send_sems.at[part, stage],
            recv_sem=recv_sems.at[part, stage],
            device_id=partner(bit),
            device_id_type=MESH,
        )
        copy.start()
        return copy

    def add(part, stage):
        free = orders[part][stage + 1 :]
        count, start = 1 << len(free), start_of(stage)
        base = fixed(part, stage + 1)

        def step(e):
            at = base + spread(e, free)
            if stage == 0:
                for k in range(group):
                    here = pl.ds(k * depth, depth)
                    got = landed[part, start + e, here, :].astype(jnp.float32)
                    mine = pl.ds(part * rows + k * depth, depth)
                    total[at, mine, :] = tap_block(part, k, at) + got
            else:
                got = landed[part, start + e].astype(jnp.float32)
                total[at, span(part), :] = total[at, span(part), :] + got

        each(count, step)

    copies = [send(part, 0) for part in range(parts)]
    for stage in range(stages):
        for part in range(parts):
            copies[part].wait_recv()
            add(part, stage)
            copies[part].wait_send()
            if stage + 1 < stages:
                copies[part] = send(part, stage + 1)
            else:
                out_ref[span(part), :] = total[fixed(part, stages), span(part), :]


def exchange(keep, send, axis, step):
    count = lax.axis_size(axis)
    got = lax.ppermute(send.astype(jnp.bfloat16), axis, [(i, i ^ step) for i in range(count)])
    return keep + got.astype(jnp.float32)


def halve_chunks(sums, axis, step):
    taps, chunks, rows, width = sums.shape
    pairs = sums.reshape(taps, chunks // 2, 2, rows, width)
    mine = lax.rem(lax.axis_index(axis) // step, 2)
    keep = lax.dynamic_index_in_dim(pairs, mine, 2, keepdims=False)
    send = lax.dynamic_index_in_dim(pairs, 1 - mine, 2, keepdims=False)
    return exchange(keep, send, axis, step)


def halve_width(sums, axis, step):
    half = sums.shape[3] // 2
    mine = lax.rem(lax.axis_index(axis) // step, 2)
    low, high = sums[..., :half], sums[..., half:]
    keep = jnp.where(mine == 0, low, high)
    send = jnp.where(mine == 0, high, low)
    return exchange(keep, send, axis, step)


def scatter_by_permutes(sums):
    bands, groups = lax.axis_size("space"), lax.axis_size("tm")
    taps, rows, width = sums.shape
    sums = sums.reshape(taps, bands, rows // bands, width)
    sums = halve_chunks(sums, "space", 1)
    step = groups // 2
    while step >= 1:
        sums = halve_width(sums, "tm", step)
        step //= 2
    step = 2
    while step < bands:
        sums = halve_chunks(sums, "space", step)
        step *= 2
    return jnp.transpose(sums[:, 0], (0, 2, 1))


def scatter_sums(terms):
    bands, groups = lax.axis_size("space"), lax.axis_size("tm")
    taps, (rows, width) = len(terms), terms[0].shape
    depth, lanes = rows // bands, width // groups
    if depth % 16 or lanes != 128 or taps % 3:
        return scatter_by_permutes(jnp.stack(terms))
    orders = bit_orders(bands, groups)
    parts, stages, devices = len(orders), len(orders[0]), bands * groups
    lines = taps * depth
    owned = pl.pallas_call(
        functools.partial(scatter_kernel, orders, depth, lanes),
        out_shape=jax.ShapeDtypeStruct((lines, 128), jnp.float32),
        in_specs=[pl.BlockSpec(memory_space=pltpu.VMEM)] * taps,
        out_specs=pl.BlockSpec(memory_space=pltpu.VMEM),
        scratch_shapes=[
            pltpu.VMEM((devices, lines, 128), jnp.float32),
            pltpu.VMEM((parts, devices, lines // parts, 128), jnp.bfloat16),
            pltpu.VMEM((parts, devices, lines // parts, 128), jnp.bfloat16),
            pltpu.SemaphoreType.DMA((parts, stages)),
            pltpu.SemaphoreType.DMA((parts, stages)),
        ],
        compiler_params=pltpu.CompilerParams(
            collective_id=0, has_side_effects=True, vmem_limit_bytes=16 * 1024 * 1024
        ),
    )(*terms)
    return jnp.transpose(owned.reshape(taps, depth, lanes), (0, 2, 1))


def body(frames_in, w_space, w_time, grad_out):
    count, height, width, chans = frames_in.shape
    groups = lax.axis_size("tm")
    onward = [(i, i + 1) for i in range(groups - 1)]
    grad_next = lax.ppermute(grad_out[:2], "tm", [(t, s) for s, t in onward])
    extended = pad_columns(extended_2(frames_in, (("space", 1),), 1))
    pre = jnp.zeros((count * height * width, chans), jnp.float32)
    for i in range(3):
        for j in range(3):
            window = extended[:, i : i + height, j : j + width].reshape(-1, chans)
            pre = pre + jnp.dot(window, w_space[3 * i + j], preferred_element_type=jnp.float32)
    pre = rows_major(pre.reshape(count, height, width, chans))
    hidden = rows_major(jax.nn.silu(pre).astype(jnp.bfloat16))
    past = lax.ppermute(hidden[count - 2 :], "tm", onward)
    grad_hidden = temporal_backward(
        jnp.concatenate([grad_out, grad_next], axis=0), w_time, count
    )
    sig = jax.nn.sigmoid(pre)
    grad_pre = (grad_hidden.astype(jnp.float32) * sig * (1.0 + pre * (1.0 - sig))).astype(
        jnp.bfloat16
    )
    grad_pre = rows_major(grad_pre)
    grad_ext_rows = rows_major(pad_columns(extended_2(grad_pre, (("space", 1),), 1)))
    flat_pre = grad_pre.reshape(-1, chans)
    terms = []
    for i in range(3):
        for j in range(3):
            source = extended[:, i : i + height, j : j + width].reshape(-1, chans)
            terms.append(
                lax.dot_general(
                    flat_pre, source, (((0,), (0,)), ((), ())), preferred_element_type=jnp.float32
                )
            )
    block_out, time_terms = temporal_forward(
        jnp.concatenate([past, hidden], axis=0), grad_out, w_time
    )
    owned = scatter_sums(terms + time_terms)
    back = jnp.zeros((count * height * width, chans), jnp.float32)
    for i in range(3):
        for j in range(3):
            window = grad_ext_rows[:, 2 - i : 2 - i + height, 2 - j : 2 - j + width].reshape(
                -1, chans
            )
            back = back + lax.dot_general(
                window,
                w_space[3 * i + j],
                (((1,), (1,)), ((), ())),
                preferred_element_type=jnp.float32,
            )
    grad_in = back.reshape(count, height, width, chans).astype(jnp.bfloat16)
    return (block_out, grad_in, owned[:9], owned[9:])


def solution(mesh):
    in_specs = (P("tm", "space", None, None), P(), P(), P("tm", "space", None, None))
    out_specs = (
        P("tm", "space", None, None),
        P("tm", "space", None, None),
        P(None, "tm", "space"),
        P(None, "tm", "space"),
    )
    return jax.shard_map(body, mesh=mesh, in_specs=in_specs, out_specs=out_specs, check_vma=False)
```

```python
import functools

import jax
import jax.numpy as jnp
from jax import lax
from jax.experimental import pallas as pl
from jax.experimental.layout import Layout, with_layout_constraint
from jax.experimental.pallas import tpu as pltpu
from jax.sharding import PartitionSpec as P


def extended_2(block, sides, width):
    for axis, dim in sides:
        count = lax.axis_size(axis)
        forward = [(i, i + 1) for i in range(count - 1)]
        backward = [(target, source) for source, target in forward]
        low = lax.ppermute(
            lax.slice_in_dim(block, block.shape[dim] - width, None, axis=dim), axis, forward
        )
        high = lax.ppermute(lax.slice_in_dim(block, 0, width, axis=dim), axis, backward)
        block = jnp.concatenate([low, block, high], axis=dim)
    return block


def pad_columns(field):
    return jnp.pad(field, ((0, 0), (0, 0), (1, 1), (0, 0)))


def temporal_forward(past_ext, grad, w_time):
    count, chans = grad.shape[0], grad.shape[-1]
    flat_grad = grad.reshape(-1, chans)
    out_sum = jnp.zeros(flat_grad.shape, jnp.float32)
    filters = []
    for k in range(3):
        source = past_ext[k : k + count].reshape(-1, chans)
        out_sum = out_sum + jnp.dot(source, w_time[k], preferred_element_type=jnp.float32)
        filters.append(
            lax.dot_general(
                flat_grad, source, (((0,), (0,)), ((), ())), preferred_element_type=jnp.float32
            )
        )
    return out_sum.reshape(grad.shape).astype(jnp.bfloat16), filters


def temporal_backward(grad_ext, w_time, count):
    chans = grad_ext.shape[-1]
    back_sum = jnp.zeros((grad_ext[0:count].size // chans, chans), jnp.float32)
    for k in range(3):
        later = grad_ext[2 - k : 2 - k + count].reshape(-1, chans)
        back_sum = back_sum + lax.dot_general(
            later, w_time[k], (((1,), (1,)), ((), ())), preferred_element_type=jnp.float32
        )
    return back_sum.reshape(grad_ext[0:count].shape).astype(jnp.bfloat16)


MESH = pl.DeviceIdType.MESH


def rows_major(field):
    return with_layout_constraint(field, Layout(tuple(range(field.ndim))))


def bit_orders(bands, groups):
    frame_bits = [("tm", 1 << i, 1 << i) for i in range(groups.bit_length() - 1)]
    row_bits = [("space", 1 << i, groups << i) for i in range(bands.bit_length() - 1)]
    first, second, rest = row_bits[:1], row_bits[1:2], row_bits[2:]
    return [
        first + frame_bits + second + rest,
        first + second + rest + frame_bits,
        first + rest + frame_bits + second,
    ]


def side(bit):
    axis, step, _ = bit
    return lax.rem(lax.axis_index(axis) // step, 2)


def partner(bit):
    axis, step, _ = bit
    at = {"tm": lax.axis_index("tm"), "space": lax.axis_index("space")}
    at[axis] = at[axis] + step - 2 * step * side(bit)
    return (at["tm"], at["space"])


def each(count, step):
    if count <= 16:
        for e in range(count):
            step(e)
    else:
        lax.fori_loop(0, count, lambda e, carry: (step(e), carry)[1], 0)


def spread(e, free):
    if isinstance(e, int):
        return sum(((e >> i) % 2) * bit[2] for i, bit in enumerate(free))
    total = 0
    for i, bit in enumerate(free):
        total = total + lax.rem(e // (1 << i), 2) * bit[2]
    return total


def scatter_kernel(orders, depth, lanes, *refs):
    taps = len(refs) - 6
    tap_refs = refs[:taps]
    out_ref, total, sent, landed, send_sems, recv_sems = refs[taps:]
    parts = len(orders)
    group = taps // parts
    rows = group * depth
    groups = lax.axis_size("tm")
    stages = len(orders[0])
    barrier = pltpu.get_barrier_semaphore()
    for bit in orders[0]:
        pl.semaphore_signal(barrier, inc=1, device_id=partner(bit), device_id_type=MESH)

    def span(part):
        return pl.ds(part * rows, rows)

    def tap_block(part, k, at):
        down = pl.multiple_of((at // groups) * depth, depth)
        across = pl.multiple_of(lax.rem(at, groups) * lanes, lanes)
        return tap_refs[part * group + k][pl.ds(down, depth), pl.ds(across, lanes)]

    def start_of(stage):
        return sum(1 << (stages - 1 - s) for s in range(stage))

    def fixed(part, stage):
        return sum(side(bit) * bit[2] for bit in orders[part][:stage])

    def send(part, stage):
        bit, free = orders[part][stage], orders[part][stage + 1 :]
        count, start = 1 << len(free), start_of(stage)
        base = fixed(part, stage) + (1 - side(bit)) * bit[2]

        def pack(e):
            at = base + spread(e, free)
            if stage == 0:
                for k in range(group):
                    block = tap_block(part, k, at)
                    sent[part, start + e, pl.ds(k * depth, depth), :] = block.astype(jnp.bfloat16)
            else:
                sent[part, start + e] = total[at, span(part), :].astype(jnp.bfloat16)

        each(count, pack)
        return pltpu.make_async_remote_copy(
            src_ref=sent.at[part, pl.ds(start, count)],
            dst_ref=landed.at[part, pl.ds(start, count)],
            send_sem=send_sems.at[part, stage],
            recv_sem=recv_sems.at[part, stage],
            device_id=partner(bit),
            device_id_type=MESH,
        )

    def add(part, stage):
        free = orders[part][stage + 1 :]
        count, start = 1 << len(free), start_of(stage)
        base = fixed(part, stage + 1)

        def step(e):
            at = base + spread(e, free)
            if stage == 0:
                for k in range(group):
                    here = pl.ds(k * depth, depth)
                    got = landed[part, start + e, here, :].astype(jnp.float32)
                    mine = pl.ds(part * rows + k * depth, depth)
                    total[at, mine, :] = tap_block(part, k, at) + got
            else:
                got = landed[part, start + e].astype(jnp.float32)
                total[at, span(part), :] = total[at, span(part), :] + got

        each(count, step)

    copies = [send(part, 0) for part in range(parts)]
    pl.semaphore_wait(barrier, stages)
    for copy in copies:
        copy.start()
    started = list(copies)
    for stage in range(stages):
        for part in range(parts):
            copies[part].wait_recv()
            add(part, stage)
            if stage + 1 < stages:
                copies[part] = send(part, stage + 1)
                copies[part].start()
                started.append(copies[part])
            else:
                out_ref[span(part), :] = total[fixed(part, stages), span(part), :]
    for copy in started:
        copy.wait_send()


def exchange(keep, send, axis, step):
    count = lax.axis_size(axis)
    got = lax.ppermute(send.astype(jnp.bfloat16), axis, [(i, i ^ step) for i in range(count)])
    return keep + got.astype(jnp.float32)


def halve_chunks(sums, axis, step):
    taps, chunks, rows, width = sums.shape
    pairs = sums.reshape(taps, chunks // 2, 2, rows, width)
    mine = lax.rem(lax.axis_index(axis) // step, 2)
    keep = lax.dynamic_index_in_dim(pairs, mine, 2, keepdims=False)
    send = lax.dynamic_index_in_dim(pairs, 1 - mine, 2, keepdims=False)
    return exchange(keep, send, axis, step)


def halve_width(sums, axis, step):
    half = sums.shape[3] // 2
    mine = lax.rem(lax.axis_index(axis) // step, 2)
    low, high = sums[..., :half], sums[..., half:]
    keep = jnp.where(mine == 0, low, high)
    send = jnp.where(mine == 0, high, low)
    return exchange(keep, send, axis, step)


def scatter_by_permutes(sums):
    bands, groups = lax.axis_size("space"), lax.axis_size("tm")
    taps, rows, width = sums.shape
    sums = sums.reshape(taps, bands, rows // bands, width)
    sums = halve_chunks(sums, "space", 1)
    step = groups // 2
    while step >= 1:
        sums = halve_width(sums, "tm", step)
        step //= 2
    step = 2
    while step < bands:
        sums = halve_chunks(sums, "space", step)
        step *= 2
    return jnp.transpose(sums[:, 0], (0, 2, 1))


def scatter_sums(terms):
    bands, groups = lax.axis_size("space"), lax.axis_size("tm")
    taps, (rows, width) = len(terms), terms[0].shape
    depth, lanes = rows // bands, width // groups
    if depth % 16 or lanes != 128 or taps % 3:
        return scatter_by_permutes(jnp.stack(terms))
    orders = bit_orders(bands, groups)
    parts, stages, devices = len(orders), len(orders[0]), bands * groups
    lines = taps * depth
    owned = pl.pallas_call(
        functools.partial(scatter_kernel, orders, depth, lanes),
        out_shape=jax.ShapeDtypeStruct((lines, 128), jnp.float32),
        in_specs=[pl.BlockSpec(memory_space=pltpu.VMEM)] * taps,
        out_specs=pl.BlockSpec(memory_space=pltpu.VMEM),
        scratch_shapes=[
            pltpu.VMEM((devices, lines, 128), jnp.float32),
            pltpu.VMEM((parts, devices, lines // parts, 128), jnp.bfloat16),
            pltpu.VMEM((parts, devices, lines // parts, 128), jnp.bfloat16),
            pltpu.SemaphoreType.DMA((parts, stages)),
            pltpu.SemaphoreType.DMA((parts, stages)),
        ],
        compiler_params=pltpu.CompilerParams(
            collective_id=0, has_side_effects=True, vmem_limit_bytes=16 * 1024 * 1024
        ),
    )(*terms)
    return jnp.transpose(owned.reshape(taps, depth, lanes), (0, 2, 1))


def body(frames_in, w_space, w_time, grad_out):
    count, height, width, chans = frames_in.shape
    groups = lax.axis_size("tm")
    onward = [(i, i + 1) for i in range(groups - 1)]
    grad_next = lax.ppermute(grad_out[:2], "tm", [(t, s) for s, t in onward])
    extended = pad_columns(extended_2(frames_in, (("space", 1),), 1))
    pre = jnp.zeros((count * height * width, chans), jnp.float32)
    for i in range(3):
        for j in range(3):
            window = extended[:, i : i + height, j : j + width].reshape(-1, chans)
            pre = pre + jnp.dot(window, w_space[3 * i + j], preferred_element_type=jnp.float32)
    pre = rows_major(pre.reshape(count, height, width, chans))
    hidden = rows_major(jax.nn.silu(pre).astype(jnp.bfloat16))
    past = lax.ppermute(hidden[count - 2 :], "tm", onward)
    grad_hidden = temporal_backward(
        jnp.concatenate([grad_out, grad_next], axis=0), w_time, count
    )
    sig = jax.nn.sigmoid(pre)
    grad_pre = (grad_hidden.astype(jnp.float32) * sig * (1.0 + pre * (1.0 - sig))).astype(
        jnp.bfloat16
    )
    grad_pre = rows_major(grad_pre)
    grad_ext_rows = rows_major(pad_columns(extended_2(grad_pre, (("space", 1),), 1)))
    flat_pre = grad_pre.reshape(-1, chans)
    terms = []
    for i in range(3):
        for j in range(3):
            source = extended[:, i : i + height, j : j + width].reshape(-1, chans)
            terms.append(
                lax.dot_general(
                    flat_pre, source, (((0,), (0,)), ((), ())), preferred_element_type=jnp.float32
                )
            )
    block_out, time_terms = temporal_forward(
        jnp.concatenate([past, hidden], axis=0), grad_out, w_time
    )
    owned = scatter_sums(terms + time_terms)
    back = jnp.zeros((count * height * width, chans), jnp.float32)
    for i in range(3):
        for j in range(3):
            window = grad_ext_rows[:, 2 - i : 2 - i + height, 2 - j : 2 - j + width].reshape(
                -1, chans
            )
            back = back + lax.dot_general(
                window,
                w_space[3 * i + j],
                (((1,), (1,)), ((), ())),
                preferred_element_type=jnp.float32,
            )
    grad_in = back.reshape(count, height, width, chans).astype(jnp.bfloat16)
    return (block_out, grad_in, owned[:9], owned[9:])


def solution(mesh):
    in_specs = (P("tm", "space", None, None), P(), P(), P("tm", "space", None, None))
    out_specs = (
        P("tm", "space", None, None),
        P("tm", "space", None, None),
        P(None, "tm", "space"),
        P(None, "tm", "space"),
    )
    return jax.shard_map(body, mesh=mesh, in_specs=in_specs, out_specs=out_specs, check_vma=False)
```
